32 devices in a mesh: dp: 8 (over z, core), group: 4 (over y, x).
Axes of the slice: x: 2, y: 2, z: 4, core: 2. Of those that a mesh axis runs over, the one named last changes fastest.
Arguments:
- attended: bfloat16 [16384, 768], P(('dp', 'group')), may hold values from -6 to 6
- cotangent: bfloat16 [16384, 1536], P(('dp', 'group')), may hold values from -6 to 6
- weight: float32 [768, 1536], P('dp'), may hold values from -0.21875 to 0.21875
- weight_first: float32 [768, 1536], P('dp'), may hold values from -0.0078125 to 0.0078125, as said below
- weight_second: float32 [768, 1536], P('dp'), may hold values from 2.44140625e-09 to 1.2207031e-06, as said below
- bias: float32 [1536], replicated, may hold values from -3 to 3
- layer_scale: float32 [1536], replicated, may hold values from 0.1 to 1, as said below
- small_first: float32 [2, 1536], replicated, may hold values from -0.0078125 to 0.0078125, as said below
- small_second: float32 [2, 1536], replicated, may hold values from 2.44140625e-09 to 1.2207031e-06, as said below
- teacher_weight: float32 [768, 1536], P('dp'), may hold values from -0.21875 to 0.21875
- teacher_bias: float32 [1536], replicated, may hold values from -3 to 3
- teacher_scale: float32 [1536], replicated, may hold values from 0.1 to 1
- teacher_attended: bfloat16 [4096, 768], P(('dp', 'group')), may hold values from -6 to 6
- teacher_resid: bfloat16 [4096, 1536], P(('dp', 'group')), may hold values from -6 to 6
Outputs:
- new_weight: float32 [768, 1536], P('dp')
- new_weight_first: float32 [768, 1536], P('dp')
- new_weight_second: float32 [768, 1536], P('dp')
- weight_direction: float32 [768, 1536], P('dp')
- new_teacher_weight: float32 [768, 1536], P('dp')
- new_small: float32 [2, 1536], replicated
- new_small_first: float32 [2, 1536], replicated
- new_small_second: float32 [2, 1536], replicated
- small_direction: float32 [2, 1536], replicated
- new_teacher_small: float32 [2, 1536], replicated
- teacher_out: bfloat16 [4096, 1536], P(('dp', 'group'))
The draws below stay inside these ranges and needn't reach their ends.
Inputs may be any that keep to these rules, and one draw needn't show every extreme that they name: `layer_scale`: LayerScale factors of a trained block. `weight_first`: moment estimates of an Adam state. `weight_second`: moment estimates of an Adam state. `small_first`: moment estimates of an Adam state. `small_second`: moment estimates of an Adam state.
All inputs are finite; a program needn't handle non-finite values.
Results may differ from the reference program's by a relative error of at most 0.0085.
Values may be sent and summed in bfloat16 or wider, within the bound.
A program may use at most 64 MiB of HBM per device.

```python
import math
import jax
import jax.numpy as jnp
from jax import lax

D = 1536
HD = 768
TOK_DEV = 512
TOKENS = 16384
TEA_TOK = 4096


def column_scales(key):
    return jnp.exp(jax.random.uniform(key, (D,), jnp.float32, math.log(0.1), math.log(1.0)))


def draw_layer_scale(key, part):
    return column_scales(key)


def draw_weight_first(key, part):
    scales = column_scales(key)
    key = jax.random.fold_in(key, 3)
    noise = jnp.clip(jax.random.normal(key, (HD, D), jnp.float32), -5.0, 5.0)
    return noise * scales[None, :] * (0.2 / TOKENS ** 0.5)


def draw_weight_second(key, part):
    scales = column_scales(key)
    key = jax.random.fold_in(key, 5)
    level = jnp.exp(jax.random.uniform(key, (HD, D), jnp.float32, math.log(0.004), math.log(0.02)))
    return level * (scales * scales)[None, :] / TOKENS


def draw_small_first(key, part):
    scales = column_scales(key)
    key = jax.random.fold_in(key, 7)
    rows = jnp.stack([scales, jnp.ones((D,), jnp.float32)])
    noise = jnp.clip(jax.random.normal(key, (2, D), jnp.float32), -5.0, 5.0)
    return noise * rows * (0.2 / TOKENS ** 0.5)


def draw_small_second(key, part):
    scales = column_scales(key)
    key = jax.random.fold_in(key, 9)
    rows = jnp.stack([scales, jnp.ones((D,), jnp.float32)])
    level = jnp.exp(jax.random.uniform(key, (2, D), jnp.float32, math.log(0.004), math.log(0.02)))
    return level * rows * rows / TOKENS


def raised(drawn, key, source, target, shards_of, factor):
    def block_of(dim):
        return (jnp.arange(drawn.shape[dim]) // (drawn.shape[dim] // shards_of)).reshape((-1,) + (1,) * (drawn.ndim - 1 - dim))

    one_side = jax.random.permutation(key, shards_of)[block_of(target)]
    other_side = (block_of(target) + shards_of // 2) % shards_of
    return jnp.where((block_of(source) == one_side) | (block_of(source) == other_side), factor * drawn, drawn)


def steps_of(stream_key, extent, cuts, low, largest):
    level = 1.0
    for dim, parts in cuts:
        draws = jax.random.uniform(jax.random.fold_in(jax.random.fold_in(stream_key, 6), dim), (parts,), jnp.float32, low / len(cuts), largest / len(cuts))
        level = level * jnp.repeat(jnp.exp(draws), extent[dim] // parts).reshape((-1,) + (1,) * (len(extent) - 1 - dim))
    return level


def normal_values(key, dims, spread, bound, split=(), dtype=jnp.bfloat16):
    drawn = jax.random.normal(key, dims, jnp.float32) * spread
    if len(split) > 0:
        drawn = steps_of(key, dims, split, -0.22, 0.18) * drawn
    return jnp.clip(drawn, min=-bound, max=bound).astype(dtype)


def heavy_noise(own_key, dims, scale, limit, shards, heavy, dtype=jnp.bfloat16):
    values = scale * jax.random.normal(own_key, dims, jnp.float32)
    if shards:
        values = values * steps_of(own_key, dims, shards, -0.22, 0.18)
    return jnp.clip(raised(values, jax.random.fold_in(own_key, 3), *heavy), -limit, limit).astype(dtype)


def setup_inputs(seed: int = 0) -> dict:
    seeds = jax.random.split(jax.random.key(seed), 15)
    return {
        "attended": heavy_noise(seeds[0], (TOKENS, HD), 1.0, 6.0, ((0, 32),), (0, 1, 32, 2.75)),
        "cotangent": normal_values(seeds[1], (TOKENS, D), 1.0, 6.0, ((0, 32),)),
        "weight": normal_values(seeds[2], (HD, D), HD ** -0.5, 0.21875, ((0, 8),), jnp.float32),
        "weight_first": draw_weight_first(jax.random.fold_in(seeds[14], 71), 0),
        "weight_second": draw_weight_second(jax.random.fold_in(seeds[14], 71), 0),
        "bias": normal_values(seeds[5], (D,), 0.5, 3.0, (), jnp.float32),
        "layer_scale": draw_layer_scale(jax.random.fold_in(seeds[14], 71), 0),
        "small_first": draw_small_first(jax.random.fold_in(seeds[14], 71), 0),
        "small_second": draw_small_second(jax.random.fold_in(seeds[14], 71), 0),
        "teacher_weight": normal_values(seeds[9], (HD, D), HD ** -0.5, 0.21875, ((0, 8),), jnp.float32),
        "teacher_bias": normal_values(seeds[10], (D,), 0.5, 3.0, (), jnp.float32),
        "teacher_scale": jnp.clip(jnp.exp(jax.random.uniform(seeds[11], (D,), jnp.float32, math.log(0.1), math.log(1.0))), 0.1, 1.0),
        "teacher_attended": normal_values(seeds[12], (TEA_TOK, HD), 1.0, 6.0, ((0, 32),)),
        "teacher_resid": normal_values(seeds[13], (TEA_TOK, D), 1.0, 6.0, ((0, 32),)),
    }


BETA_ONE = 0.9
BETA_TWO = 0.999
LEARN_RATE = 0.0004
WEIGHT_DECAY = 0.04
EPSILON = 1e-08
MOMENTUM = 0.994
CORRECT_ONE = 1.0 - 0.9 ** 10
CORRECT_TWO = 1.0 - 0.999 ** 10

def adam_update(param, first, second, grad, decay):
    first = BETA_ONE * first + (1.0 - BETA_ONE) * grad
    second = BETA_TWO * second + (1.0 - BETA_TWO) * grad * grad
    direction = first / CORRECT_ONE / (jnp.sqrt(second / CORRECT_TWO) + EPSILON) + decay * param
    return (param - LEARN_RATE * direction, first, second, direction)

def reference(attended, cotangent, weight, weight_first, weight_second, bias, layer_scale, small_first, small_second, teacher_weight, teacher_bias, teacher_scale, teacher_attended, teacher_resid):
    blocks = attended.shape[0] // TOK_DEV
    total = attended.shape[0]
    narrow = weight.astype(jnp.bfloat16)

    def accumulate(carry, pair):
        inputs, grads = pair
        part = lax.dot_general(inputs, grads, (((0,), (0,)), ((), ())), preferred_element_type=jnp.float32)
        part = lax.optimization_barrier(part.astype(jnp.bfloat16)).astype(jnp.float32)
        branch = jnp.dot(inputs, narrow, preferred_element_type=jnp.float32) + bias
        grad_rows = grads.astype(jnp.float32)
        return ((carry[0] + part, carry[1] + lax.optimization_barrier(jnp.sum(grad_rows, 0)), carry[2] + lax.optimization_barrier(jnp.sum(grad_rows * branch, 0))), None)
    start = (jnp.zeros((HD, D), jnp.float32), jnp.zeros((D,), jnp.float32), jnp.zeros((D,), jnp.float32))
    pairs = (attended.reshape(blocks, TOK_DEV, HD), cotangent.reshape(blocks, TOK_DEV, D))
    (summed, bias_sum, scale_sum), _ = lax.scan(accumulate, start, pairs)
    grad_weight = summed * layer_scale[None, :] / total
    grad_small = jnp.stack([layer_scale * bias_sum, scale_sum]) / total
    new_weight, new_weight_first, new_weight_second, weight_direction = adam_update(weight, weight_first, weight_second, grad_weight, WEIGHT_DECAY)
    small = jnp.stack([bias, layer_scale])
    new_small, new_small_first, new_small_second, small_direction = adam_update(small, small_first, small_second, grad_small, 0.0)
    new_teacher_weight = MOMENTUM * teacher_weight + (1.0 - MOMENTUM) * weight
    new_teacher_small = MOMENTUM * jnp.stack([teacher_bias, teacher_scale]) + (1.0 - MOMENTUM) * small
    teacher_branch = jnp.dot(teacher_attended, new_teacher_weight.astype(jnp.bfloat16), preferred_element_type=jnp.float32)
    teacher_out = (teacher_resid.astype(jnp.float32) + new_teacher_small[1] * (teacher_branch + new_teacher_small[0])).astype(jnp.bfloat16)
    return (new_weight, new_weight_first, new_weight_second, weight_direction, new_teacher_weight, new_small, new_small_first, new_small_second, small_direction, new_teacher_small, teacher_out)
```

```python
import functools

import jax
import jax.numpy as jnp
from jax import lax
from jax.experimental import pallas as pl
from jax.experimental.pallas import tpu as pltpu
from jax.sharding import PartitionSpec as P

BETA_ONE = 0.9
BETA_TWO = 0.999
LEARN_RATE = 0.0004
WEIGHT_DECAY = 0.04
EPSILON = 1e-08
MOMENTUM = 0.994
CORRECT_ONE = 1.0 - 0.9**10
CORRECT_TWO = 1.0 - 0.999**10
PIECES = 4
F32 = jnp.float32
BF16 = jnp.bfloat16


def adam_update(param, first, second, grad, decay):
    first = BETA_ONE * first + (1.0 - BETA_ONE) * grad
    second = BETA_TWO * second + (1.0 - BETA_TWO) * grad * grad
    direction = first / CORRECT_ONE / (jnp.sqrt(second / CORRECT_TWO) + EPSILON) + decay * param
    return (param - LEARN_RATE * direction, first, second, direction)


def exchange(
    ndp,
    ngroup,
    att_hbm,
    cot_hbm,
    weight_hbm,
    tweight_hbm,
    tatt_hbm,
    tres_hbm,
    bias_ref,
    scale_ref,
    tbias_ref,
    tscale_ref,
    grad_ref,
    sums_ref,
    tout_ref,
    att,
    cot,
    weight,
    tweight,
    tatt,
    tres,
    tgather,
    part,
    from_core,
    acc,
    narrow,
    got_a,
    got_b,
    send_a,
    send_b,
    last_a,
    last_b,
    extra_out,
    extra_in,
    z_out,
    z_in,
    pieces,
    bias_slots,
    small_slots,
    load_sem,
    t_core_sem,
    t_up_sem,
    t_down_sem,
    t_recv,
    core_send,
    core_recv,
    plane_send,
    plane_recv,
    extra_send,
    extra_recv,
    z_send,
    z_recv,
    piece_send,
    piece_recv,
    bias_send,
    bias_recv,
    small_send,
    small_recv,
):
    line = ndp // 2
    half = line // 2
    i = lax.axis_index("dp")
    g = lax.axis_index("group")
    p = i // 2
    c = i % 2
    own = g % PIECES
    rows, width = weight.shape
    wide = width // PIECES

    def flip(index, bits):
        out = index
        bit = 1
        while bit <= bits:
            if bits & bit:
                out = out + bit - 2 * bit * ((index // bit) % 2)
            bit *= 2
        return out

    def remote(src, dst, send_sem, recv_sem, dp, group):
        return pltpu.make_async_remote_copy(
            src_ref=src,
            dst_ref=dst,
            send_sem=send_sem,
            recv_sem=recv_sem,
            device_id=(dp, group),
            device_id_type=pl.DeviceIdType.MESH,
        )

    loads = [
        pltpu.make_async_copy(src, dst, load_sem.at[k])
        for k, (src, dst) in enumerate(
            [
                (tweight_hbm, tweight),
                (weight_hbm, weight),
                (att_hbm, att),
                (cot_hbm, cot),
                (tatt_hbm, tatt),
                (tres_hbm, tres),
            ]
        )
    ]
    for load in loads:
        load.start()

    barrier = pltpu.get_barrier_semaphore()
    for k in range(1, ndp):
        pl.semaphore_signal(
            barrier, inc=1, device_id=(flip(i, k), g), device_id_type=pl.DeviceIdType.MESH
        )
    for k in range(1, ngroup):
        pl.semaphore_signal(
            barrier, inc=1, device_id=(i, flip(g, k)), device_id_type=pl.DeviceIdType.MESH
        )

    loads[0].wait()
    loads[1].wait()
    blended = MOMENTUM * tweight[...] + (1.0 - MOMENTUM) * weight[...]
    tgather[i] = blended.astype(BF16)
    pl.semaphore_wait(barrier, ndp - 1 + ngroup - 1)

    def t_copy(slot, send_sem, dp):
        return remote(tgather.at[slot], tgather.at[slot], send_sem, t_recv.at[slot], dp, g)

    mate = flip(i, 1)
    up = jnp.minimum(i + 2, ndp - 1)
    down = jnp.maximum(i - 2, 0)
    has_up = p < line - 1
    has_down = p > 0

    @pl.when(has_up)
    def _():
        t_copy(i, t_up_sem.at[0], i + 2).start()

    @pl.when(has_down)
    def _():
        t_copy(i, t_down_sem.at[0], i - 2).start()

    t_copy(i, t_core_sem.at[0], mate).start()

    def forward(d):
        @pl.when(p - d >= 0)
        def _():
            slot = i - 2 * d
            t_copy(slot, t_core_sem.at[2 * d - 1], mate).wait_recv()
            t_copy(slot, t_core_sem.at[2 * d - 1], mate).start()
            if d < line - 1:

                @pl.when(has_up)
                def _():
                    t_copy(slot, t_up_sem.at[d], i + 2).start()

        @pl.when(p + d < line)
        def _():
            slot = i + 2 * d
            t_copy(slot, t_core_sem.at[2 * d], mate).wait_recv()
            t_copy(slot, t_core_sem.at[2 * d], mate).start()
            if d < line - 1:

                @pl.when(has_down)
                def _():
                    t_copy(slot, t_down_sem.at[d], i - 2).start()

    loads[2].wait()
    turned = att[...].T
    loads[3].wait()
    order = [3, 1, 2, 0]
    core_copies = []
    for k in order:
        q = flip(own, k)
        columns = pl.ds(pl.multiple_of(q * wide, wide), wide)
        product = jnp.dot(turned, cot[:, columns], preferred_element_type=F32)
        product = product.reshape(line, 2, rows, wide).astype(BF16)
        part[0, q] = product[:, 0]
        part[1, q] = product[:, 1]
        copy = remote(
            part.at[1 - c, q], from_core.at[q], core_send.at[k], core_recv.at[k], mate, g
        )
        copy.start()
        core_copies.append(copy)

    ones = jnp.ones((8, cot.shape[0]), BF16)
    bias_slots[g] = jnp.dot(ones, cot[...], preferred_element_type=F32)
    bias_copies = [
        remote(
            bias_slots.at[g], bias_slots.at[g], bias_send.at[k], bias_recv.at[k], i, flip(g, k)
        )
        for k in range(1, ngroup)
    ]
    for copy in bias_copies:
        copy.start()

    x_mate = flip(g, 1)
    y_mate = flip(g, 2)
    low = pl.ds(0, half)
    high = pl.ds(half, half)

    def plane(n, src, dst, group):
        return remote(src, dst, plane_send.at[n], plane_recv.at[n], i, group)

    plane_copies = [
        plane(0, narrow.at[flip(own, 3), low], got_a.at[0], x_mate),
        plane(1, narrow.at[flip(own, 3), high], got_b.at[0], y_mate),
        plane(2, narrow.at[flip(own, 1), low], got_a.at[1], x_mate),
        plane(3, narrow.at[flip(own, 2), high], got_b.at[1], y_mate),
        plane(4, send_a, last_a, y_mate),
        plane(5, send_b, last_b, x_mate),
    ]
    after = {3: (0, 1), 1: (2,), 2: (3,), 0: ()}
    for n, k in enumerate(order):
        q = flip(own, k)
        core_copies[n].wait_recv()
        total = part[c, q].astype(F32) + from_core[q].astype(F32)
        acc[q] = total
        if k != 0:
            narrow[q] = total.astype(BF16)
        for m in after[k]:
            plane_copies[m].start()

    forward(1)

    plane_copies[0].wait_recv()
    send_a[...] = (acc[flip(own, 2), low] + got_a[0].astype(F32)).astype(BF16)
    plane_copies[4].start()
    plane_copies[1].wait_recv()
    send_b[...] = (acc[flip(own, 1), high] + got_b[0].astype(F32)).astype(BF16)
    plane_copies[5].start()
    plane_copies[2].wait_recv()
    acc[own, low] = acc[own, low] + got_a[1].astype(F32)
    plane_copies[3].wait_recv()
    acc[own, high] = acc[own, high] + got_b[1].astype(F32)

    for d in range(2, line - 1):
        forward(d)

    for copy in bias_copies:
        copy.wait_recv()
    bias_total = bias_slots[0, 0:1]
    for k in range(1, ngroup):
        bias_total = bias_total + bias_slots[k, 0:1]
    small_slots[i, 0:1] = bias_total

    plane_copies[4].wait_recv()
    acc[own, low] = acc[own, low] + last_a[...].astype(F32)
    plane_copies[5].wait_recv()
    acc[own, high] = acc[own, high] + last_b[...].astype(F32)

    extra_copies = []
    step = 0
    while PIECES << step < ngroup:
        extra_out[step] = acc[own].astype(BF16)
        copy = remote(
            extra_out.at[step],
            extra_in.at[step],
            extra_send.at[step],
            extra_recv.at[step],
            i,
            flip(g, PIECES << step),
        )
        copy.start()
        copy.wait_recv()
        acc[own] = extra_out[step].astype(F32) + extra_in[step].astype(F32)
        extra_copies.append(copy)
        step += 1

    z_out[...] = acc[own].astype(BF16)
    z_copies = []
    for k in range(line - 1, 0, -1):
        place = flip(p, k)
        copy = remote(
            z_out.at[place], z_in.at[k - 1], z_send.at[k - 1], z_recv.at[k - 1], 2 * place + c, g
        )
        copy.start()
        z_copies.append(copy)

    if line > 2:
        forward(line - 1)
    for k in range(line):
        slot = 2 * k + 1 - c
        t_copy(slot, t_core_sem.at[0], mate).wait_recv()
    if rows % 16 == 0:
        blended_all = tgather[...].reshape(ndp * rows, width)
    else:
        blended_all = tgather[...].astype(F32).reshape(ndp * rows, width).astype(BF16)
    loads[4].wait()
    loads[5].wait()
    branch = jnp.dot(tatt[...], blended_all, preferred_element_type=F32)
    new_bias = MOMENTUM * tbias_ref[...] + (1.0 - MOMENTUM) * bias_ref[...]
    new_scale = MOMENTUM * tscale_ref[...] + (1.0 - MOMENTUM) * scale_ref[...]
    tout_ref[...] = (tres[...].astype(F32) + new_scale * (branch + new_bias)).astype(BF16)

    total = acc[own, p]
    for copy in z_copies:
        copy.wait_recv()
    for k in range(line - 1):
        total = total + z_in[k].astype(F32)
    pieces[own] = total.astype(BF16)
    piece_copies = [
        remote(
            pieces.at[own],
            pieces.at[own],
            piece_send.at[k - 1],
            piece_recv.at[k - 1],
            i,
            flip(g, k),
        )
        for k in (3, 1, 2)
    ]
    for copy in piece_copies:
        copy.start()
    for copy in piece_copies:
        copy.wait_recv()
    for q in range(PIECES):
        columns = pl.ds(q * wide, wide)
        piece = pieces[q]
        grad_ref[:, columns] = piece
        rounded = weight[:, columns].astype(BF16).astype(F32)
        small_slots[i, 1:2, columns] = jnp.sum(rounded * piece.astype(F32), 0, keepdims=True)
    small_copies = [
        remote(
            small_slots.at[i],
            small_slots.at[i],
            small_send.at[k - 1],
            small_recv.at[k - 1],
            flip(i, k),
            g,
        )
        for k in range(1, ndp)
    ]
    for copy in small_copies:
        copy.start()
    for copy in small_copies:
        copy.wait_recv()
    sums = small_slots[0]
    for k in range(1, ndp):
        sums = sums + small_slots[k]
    sums_ref[0:1] = sums[0:1]
    sums_ref[1:2] = sums[1:2] + bias_ref[...] * sums[0:1]

    for copy in (
        core_copies + bias_copies + plane_copies + extra_copies + z_copies + piece_copies
    ):
        copy.wait_send()
    for copy in small_copies:
        copy.wait_send()
    t_copy(i, t_core_sem.at[0], mate).wait_send()

    @pl.when(has_up)
    def _():
        t_copy(i, t_up_sem.at[0], i + 2).wait_send()

    @pl.when(has_down)
    def _():
        t_copy(i, t_down_sem.at[0], i - 2).wait_send()

    for d in range(1, line):

        @pl.when(p - d >= 0)
        def _(d=d):
            slot = i - 2 * d
            t_copy(slot, t_core_sem.at[2 * d - 1], mate).wait_send()
            if d < line - 1:

                @pl.when(has_up)
                def _():
                    t_copy(slot, t_up_sem.at[d], i + 2).wait_send()

        @pl.when(p + d < line)
        def _(d=d):
            slot = i + 2 * d
            t_copy(slot, t_core_sem.at[2 * d], mate).wait_send()
            if d < line - 1:

                @pl.when(has_down)
                def _():
                    t_copy(slot, t_down_sem.at[d], i - 2).wait_send()


def local(
    ndp,
    ngroup,
    attended,
    cotangent,
    weight,
    weight_first,
    weight_second,
    bias,
    layer_scale,
    small_first,
    small_second,
    teacher_weight,
    teacher_bias,
    teacher_scale,
    teacher_attended,
    teacher_resid,
):
    total = attended.shape[0] * ndp * ngroup
    rows, width = weight.shape
    line = ndp // 2
    half = line // 2
    wide = width // PIECES
    extra = max(1, (ngroup // PIECES).bit_length() - 1)
    dma = pltpu.SemaphoreType.DMA
    anywhere = pl.BlockSpec(memory_space=pl.ANY)
    vmem = pl.BlockSpec(memory_space=pltpu.VMEM)
    summed, sums, teacher_out = pl.pallas_call(
        functools.partial(exchange, ndp, ngroup),
        out_shape=(
            jax.ShapeDtypeStruct((rows, width), BF16),
            jax.ShapeDtypeStruct((2, width), F32),
            jax.ShapeDtypeStruct(teacher_resid.shape, BF16),
        ),
        in_specs=[anywhere] * 6 + [vmem] * 4,
        out_specs=[vmem] * 3,
        scratch_shapes=[
            pltpu.VMEM(attended.shape, BF16),
            pltpu.VMEM(cotangent.shape, BF16),
            pltpu.VMEM((rows, width), F32),
            pltpu.VMEM((rows, width), F32),
            pltpu.VMEM(teacher_attended.shape, BF16),
            pltpu.VMEM(teacher_resid.shape, BF16),
            pltpu.VMEM((ndp, rows, width), BF16),
            pltpu.VMEM((2, PIECES, line, rows, wide), BF16),
            pltpu.VMEM((PIECES, line, rows, wide), BF16),
            pltpu.VMEM((PIECES, line, rows, wide), F32),
            pltpu.VMEM((PIECES, line, rows, wide), BF16),
            pltpu.VMEM((2, half, rows, wide), BF16),
            pltpu.VMEM((2, half, rows, wide), BF16),
            pltpu.VMEM((half, rows, wide), BF16),
            pltpu.VMEM((half, rows, wide), BF16),
            pltpu.VMEM((half, rows, wide), BF16),
            pltpu.VMEM((half, rows, wide), BF16),
            pltpu.VMEM((extra, line, rows, wide), BF16),
            pltpu.VMEM((extra, line, rows, wide), BF16),
            pltpu.VMEM((line, rows, wide), BF16),
            pltpu.VMEM((line - 1, rows, wide), BF16),
            pltpu.VMEM((PIECES, rows, wide), BF16),
            pltpu.VMEM((ngroup, 8, width), F32),
            pltpu.VMEM((ndp, 2, width), F32),
            dma((6,)),
            dma((2 * line,)),
            dma((line,)),
            dma((line,)),
            dma((ndp,)),
            dma((PIECES,)),
            dma((PIECES,)),
            dma((6,)),
            dma((6,)),
            dma((extra,)),
            dma((extra,)),
            dma((line - 1,)),
            dma((line - 1,)),
            dma((PIECES - 1,)),
            dma((PIECES - 1,)),
            dma((ngroup,)),
            dma((ngroup,)),
            dma((ndp - 1,)),
            dma((ndp - 1,)),
        ],
        compiler_params=pltpu.CompilerParams(
            collective_id=0, has_side_effects=True, vmem_limit_bytes=40 * 1024 * 1024
        ),
    )(
        attended,
        cotangent,
        weight,
        teacher_weight,
        teacher_attended,
        teacher_resid,
        bias[None, :],
        layer_scale[None, :],
        teacher_bias[None, :],
        teacher_scale[None, :],
    )
    grad_weight = summed.astype(F32) * layer_scale[None, :] / total
    grad_small = jnp.stack([layer_scale * sums[0], sums[1]]) / total
    new_weight, new_weight_first, new_weight_second, weight_direction = adam_update(
        weight, weight_first, weight_second, grad_weight, WEIGHT_DECAY
    )
    small = jnp.stack([bias, layer_scale])
    new_small, new_small_first, new_small_second, small_direction = adam_update(
        small, small_first, small_second, grad_small, 0.0
    )
    new_teacher_weight = MOMENTUM * teacher_weight + (1.0 - MOMENTUM) * weight
    new_teacher_small = (
        MOMENTUM * jnp.stack([teacher_bias, teacher_scale]) + (1.0 - MOMENTUM) * small
    )
    return (
        new_weight,
        new_weight_first,
        new_weight_second,
        weight_direction,
        new_teacher_weight,
        new_small,
        new_small_first,
        new_small_second,
        small_direction,
        new_teacher_small,
        teacher_out,
    )


def solution(mesh):
    placed = (
        P(("dp", "group"), None),
        P(("dp", "group"), None),
        P("dp", None),
        P("dp", None),
        P("dp", None),
        P(),
        P(),
        P(),
        P(),
        P("dp", None),
        P(),
        P(),
        P(("dp", "group"), None),
        P(("dp", "group"), None),
    )
    return jax.shard_map(
        functools.partial(local, mesh.shape["dp"], mesh.shape["group"]),
        mesh=mesh,
        in_specs=placed,
        out_specs=(
            P("dp", None),
            P("dp", None),
            P("dp", None),
            P("dp", None),
            P("dp", None),
            P(),
            P(),
            P(),
            P(),
            P(),
            P(("dp", "group"), None),
        ),
        check_vma=False,
    )
```

```python
import functools

import jax
import jax.numpy as jnp
from jax import lax
from jax.experimental import pallas as pl
from jax.experimental.pallas import tpu as pltpu
from jax.sharding import PartitionSpec as P

BETA_ONE = 0.9
BETA_TWO = 0.999
LEARN_RATE = 0.0004
WEIGHT_DECAY = 0.04
EPSILON = 1e-08
MOMENTUM = 0.994
CORRECT_ONE = 1.0 - 0.9**10
CORRECT_TWO = 1.0 - 0.999**10
PIECES = 4
F32 = jnp.float32
BF16 = jnp.bfloat16


def adam_update(param, first, second, grad, decay):
    first = BETA_ONE * first + (1.0 - BETA_ONE) * grad
    second = BETA_TWO * second + (1.0 - BETA_TWO) * grad * grad
    direction = first / CORRECT_ONE / (jnp.sqrt(second / CORRECT_TWO) + EPSILON) + decay * param
    return (param - LEARN_RATE * direction, first, second, direction)


def finish(
    total,
    grad_ref,
    sums_ref,
    branch_ref,
    weight_ref,
    first_ref,
    second_ref,
    bias_ref,
    scale_ref,
    small_first_ref,
    small_second_ref,
    tweight_ref,
    tbias_ref,
    tscale_ref,
    tres_ref,
    *rest,
):
    outs, held, sem = rest[:11], rest[11:22], rest[22]
    rows, width = weight_ref.shape
    chunk = rows // 3 if rows % 24 == 0 else rows
    chunks = rows // chunk
    copies = []

    def send(n, where=None, k=0):
        src, dst = held[n], outs[n]
        if where is not None:
            src, dst = src.at[where], dst.at[where]
        copy = pltpu.make_async_copy(src, dst, sem.at[n, k])
        copy.start()
        copies.append(copy)

    scale = scale_ref[...][None, :]
    for k in range(chunks):
        where = pl.ds(k * chunk, chunk)
        grad = grad_ref[where] * scale / total
        param = weight_ref[where]
        held[4][where] = MOMENTUM * tweight_ref[where] + (1.0 - MOMENTUM) * param
        results = adam_update(param, first_ref[where], second_ref[where], grad, WEIGHT_DECAY)
        for n, result in enumerate(results):
            held[n][where] = result
        for n in range(5):
            send(n, where, k)
    bias = bias_ref[...][None, :]
    small = (bias, scale)
    bias_sum = sums_ref[0:1]
    scale_sum = sums_ref[1:2] + bias * bias_sum
    small_grad = (scale * bias_sum / total, scale_sum / total)
    blended = []
    for r, old in enumerate((tbias_ref, tscale_ref)):
        row = pl.ds(r, 1)
        results = adam_update(
            small[r], small_first_ref[row], small_second_ref[row], small_grad[r], 0.0
        )
        blended.append(MOMENTUM * old[...][None, :] + (1.0 - MOMENTUM) * small[r])
        for n, result in enumerate((*results, blended[r])):
            held[5 + n][row] = result
    for n in range(5, 10):
        send(n)
    held[10][...] = (
        tres_ref[...].astype(F32) + blended[1] * (branch_ref[...] + blended[0])
    ).astype(BF16)
    send(10)
    for copy in copies:
        copy.wait()


def exchange(
    ndp,
    ngroup,
    weight_hbm,
    tweight_hbm,
    att_hbm,
    cot_hbm,
    tatt_hbm,
    grad_ref,
    sums_ref,
    branch_ref,
    weight,
    tweight,
    att,
    cot,
    tatt,
    load_sem,
    tgather,
    part,
    from_core,
    acc,
    narrow,
    got_a,
    got_b,
    send_a,
    send_b,
    last_a,
    last_b,
    extra_out,
    extra_in,
    z_out,
    z_in,
    pieces,
    bias_slots,
    bias_all,
    scale_slots,
    scale_pieces,
    t_core_sem,
    t_up_sem,
    t_down_sem,
    t_recv,
    core_send,
    core_recv,
    plane_send,
    plane_recv,
    extra_send,
    extra_recv,
    z_send,
    z_recv,
    piece_send,
    piece_recv,
    bias_send,
    bias_recv,
    bias_all_send,
    bias_all_recv,
    scale_send,
    scale_recv,
    scale_piece_send,
    scale_piece_recv,
):
    line = ndp // 2
    half = line // 2
    i = lax.axis_index("dp")
    g = lax.axis_index("group")
    p = i // 2
    c = i % 2
    own = g % PIECES
    rows, width = weight.shape
    wide = width // PIECES

    def flip(index, bits):
        out = index
        bit = 1
        while bit <= bits:
            if bits & bit:
                out = out + bit - 2 * bit * ((index // bit) % 2)
            bit *= 2
        return out

    def remote(src, dst, send_sem, recv_sem, dp, group):
        return pltpu.make_async_remote_copy(
            src_ref=src,
            dst_ref=dst,
            send_sem=send_sem,
            recv_sem=recv_sem,
            device_id=(dp, group),
            device_id_type=pl.DeviceIdType.MESH,
        )

    loads = [
        pltpu.make_async_copy(src, dst, load_sem.at[k])
        for k, (src, dst) in enumerate(
            [
                (weight_hbm, weight),
                (tweight_hbm, tweight),
                (att_hbm, att),
                (cot_hbm, cot),
                (tatt_hbm, tatt),
            ]
        )
    ]
    for load in loads:
        load.start()

    barrier = pltpu.get_barrier_semaphore()
    for k in range(1, ndp):
        pl.semaphore_signal(
            barrier, inc=1, device_id=(flip(i, k), g), device_id_type=pl.DeviceIdType.MESH
        )
    for k in range(1, ngroup):
        pl.semaphore_signal(
            barrier, inc=1, device_id=(i, flip(g, k)), device_id_type=pl.DeviceIdType.MESH
        )

    loads[0].wait()
    loads[1].wait()
    tgather[i] = (MOMENTUM * tweight[...] + (1.0 - MOMENTUM) * weight[...]).astype(BF16)
    pl.semaphore_wait(barrier, ndp - 1 + ngroup - 1)

    def t_copy(slot, send_sem, dp):
        return remote(tgather.at[slot], tgather.at[slot], send_sem, t_recv.at[slot], dp, g)

    mate = flip(i, 1)
    up = jnp.minimum(i + 2, ndp - 1)
    down = jnp.maximum(i - 2, 0)
    has_up = p < line - 1
    has_down = p > 0

    @pl.when(has_up)
    def _():
        t_copy(i, t_up_sem.at[0], i + 2).start()

    @pl.when(has_down)
    def _():
        t_copy(i, t_down_sem.at[0], i - 2).start()

    t_copy(i, t_core_sem.at[0], mate).start()

    def forward(d):
        @pl.when(p - d >= 0)
        def _():
            slot = i - 2 * d
            t_copy(slot, t_core_sem.at[2 * d - 1], mate).wait_recv()
            t_copy(slot, t_core_sem.at[2 * d - 1], mate).start()
            if d < line - 1:

                @pl.when(has_up)
                def _():
                    t_copy(slot, t_up_sem.at[d], i + 2).start()

        @pl.when(p + d < line)
        def _():
            slot = i + 2 * d
            t_copy(slot, t_core_sem.at[2 * d], mate).wait_recv()
            t_copy(slot, t_core_sem.at[2 * d], mate).start()
            if d < line - 1:

                @pl.when(has_down)
                def _():
                    t_copy(slot, t_down_sem.at[d], i - 2).start()

    loads[2].wait()
    turned = att[...].T
    loads[3].wait()

    order = [3, 1, 2, 0]
    core_copies = []
    for k in order:
        q = flip(own, k)
        columns = pl.ds(pl.multiple_of(q * wide, wide), wide)
        product = jnp.dot(turned, cot[:, columns], preferred_element_type=F32)
        product = product.reshape(line, 2, rows, wide).astype(BF16)
        part[0, q] = product[:, 0]
        part[1, q] = product[:, 1]
        copy = remote(
            part.at[1 - c, q], from_core.at[q], core_send.at[k], core_recv.at[k], mate, g
        )
        copy.start()
        core_copies.append(copy)

    ones = jnp.ones((8, cot.shape[0]), BF16)
    bias_slots[g] = jnp.dot(ones, cot[...], preferred_element_type=F32)
    bias_copies = [
        remote(
            bias_slots.at[g], bias_slots.at[g], bias_send.at[k], bias_recv.at[k], i, flip(g, k)
        )
        for k in range(1, ngroup)
    ]
    for copy in bias_copies:
        copy.start()

    x_mate = flip(g, 1)
    y_mate = flip(g, 2)
    low = pl.ds(0, half)
    high = pl.ds(half, half)

    def plane(n, src, dst, group):
        return remote(src, dst, plane_send.at[n], plane_recv.at[n], i, group)

    plane_copies = [
        plane(0, narrow.at[flip(own, 3), low], got_a.at[0], x_mate),
        plane(1, narrow.at[flip(own, 3), high], got_b.at[0], y_mate),
        plane(2, narrow.at[flip(own, 1), low], got_a.at[1], x_mate),
        plane(3, narrow.at[flip(own, 2), high], got_b.at[1], y_mate),
        plane(4, send_a, last_a, y_mate),
        plane(5, send_b, last_b, x_mate),
    ]
    after = {3: (0, 1), 1: (2,), 2: (3,), 0: ()}
    for n, k in enumerate(order):
        q = flip(own, k)
        core_copies[n].wait_recv()
        total = part[c, q].astype(F32) + from_core[q].astype(F32)
        acc[q] = total
        if k != 0:
            narrow[q] = total.astype(BF16)
        for m in after[k]:
            plane_copies[m].start()

    forward(1)

    plane_copies[0].wait_recv()
    send_a[...] = (acc[flip(own, 2), low] + got_a[0].astype(F32)).astype(BF16)
    plane_copies[4].start()
    plane_copies[1].wait_recv()
    send_b[...] = (acc[flip(own, 1), high] + got_b[0].astype(F32)).astype(BF16)
    plane_copies[5].start()
    plane_copies[2].wait_recv()
    acc[own, low] = acc[own, low] + got_a[1].astype(F32)
    plane_copies[3].wait_recv()
    acc[own, high] = acc[own, high] + got_b[1].astype(F32)

    for d in range(2, line - 1):
        forward(d)

    for copy in bias_copies:
        copy.wait_recv()
    bias_total = bias_slots[0, 0:1]
    for k in range(1, ngroup):
        bias_total = bias_total + bias_slots[k, 0:1]
    bias_all[i] = bias_total
    bias_all_copies = [
        remote(
            bias_all.at[i],
            bias_all.at[i],
            bias_all_send.at[k - 1],
            bias_all_recv.at[k - 1],
            flip(i, k),
            g,
        )
        for k in range(1, ndp)
    ]
    for copy in bias_all_copies:
        copy.start()

    plane_copies[4].wait_recv()
    acc[own, low] = acc[own, low] + last_a[...].astype(F32)
    plane_copies[5].wait_recv()
    acc[own, high] = acc[own, high] + last_b[...].astype(F32)

    extra_copies = []
    step = 0
    while PIECES << step < ngroup:
        extra_out[step] = acc[own].astype(BF16)
        copy = remote(
            extra_out.at[step],
            extra_in.at[step],
            extra_send.at[step],
            extra_recv.at[step],
            i,
            flip(g, PIECES << step),
        )
        copy.start()
        copy.wait_recv()
        acc[own] = extra_out[step].astype(F32) + extra_in[step].astype(F32)
        extra_copies.append(copy)
        step += 1

    z_out[...] = acc[own].astype(BF16)
    z_copies = []
    for k in range(line - 1, 0, -1):
        place = flip(p, k)
        copy = remote(
            z_out.at[place], z_in.at[k - 1], z_send.at[k - 1], z_recv.at[k - 1], 2 * place + c, g
        )
        copy.start()
        z_copies.append(copy)

    if line > 2:
        forward(line - 1)
    for k in range(line):
        slot = 2 * k + 1 - c
        t_copy(slot, t_core_sem.at[0], mate).wait_recv()
    if rows % 16 == 0:
        blended_all = tgather[...].reshape(ndp * rows, width)
    else:
        blended_all = tgather[...].astype(F32).reshape(ndp * rows, width).astype(BF16)
    loads[4].wait()
    branch_ref[...] = jnp.dot(tatt[...], blended_all, preferred_element_type=F32)

    total = acc[own, p]
    for copy in z_copies:
        copy.wait_recv()
    for k in range(line - 1):
        total = total + z_in[k].astype(F32)
    pieces[own] = total.astype(BF16)
    piece_copies = [
        remote(
            pieces.at[own],
            pieces.at[own],
            piece_send.at[k - 1],
            piece_recv.at[k - 1],
            i,
            flip(g, k),
        )
        for k in (3, 1, 2)
    ]
    for copy in piece_copies:
        copy.start()
    columns = pl.ds(pl.multiple_of(own * wide, wide), wide)
    rounded = weight[:, columns].astype(BF16).astype(F32)
    scale_slots[i] = jnp.sum(rounded * pieces[own].astype(F32), 0, keepdims=True)
    scale_copies = [
        remote(
            scale_slots.at[i],
            scale_slots.at[i],
            scale_send.at[k - 1],
            scale_recv.at[k - 1],
            flip(i, k),
            g,
        )
        for k in range(ndp - 1, 0, -1)
    ]
    for copy in scale_copies:
        copy.start()
    for copy in bias_all_copies:
        copy.wait_recv()
    bias_sum = bias_all[0]
    for k in range(1, ndp):
        bias_sum = bias_sum + bias_all[k]
    sums_ref[0:1] = bias_sum
    for copy in scale_copies:
        copy.wait_recv()
    scale_sum = scale_slots[0]
    for k in range(1, ndp):
        scale_sum = scale_sum + scale_slots[k]
    scale_pieces[own] = scale_sum
    scale_piece_copies = [
        remote(
            scale_pieces.at[own],
            scale_pieces.at[own],
            scale_piece_send.at[k - 1],
            scale_piece_recv.at[k - 1],
            i,
            flip(g, k),
        )
        for k in (3, 1, 2)
    ]
    for copy in scale_piece_copies:
        copy.start()
    for copy in piece_copies:
        copy.wait_recv()
    for q in range(PIECES):
        grad_ref[:, pl.ds(q * wide, wide)] = pieces[q].astype(F32)
    for copy in scale_piece_copies:
        copy.wait_recv()
    for q in range(PIECES):
        sums_ref[1:2, pl.ds(q * wide, wide)] = scale_pieces[q]

    for copy in (
        core_copies + bias_copies + plane_copies + extra_copies + z_copies + piece_copies
    ):
        copy.wait_send()
    for copy in bias_all_copies + scale_copies + scale_piece_copies:
        copy.wait_send()
    t_copy(i, t_core_sem.at[0], mate).wait_send()

    @pl.when(has_up)
    def _():
        t_copy(i, t_up_sem.at[0], i + 2).wait_send()

    @pl.when(has_down)
    def _():
        t_copy(i, t_down_sem.at[0], i - 2).wait_send()

    for d in range(1, line):

        @pl.when(p - d >= 0)
        def _(d=d):
            slot = i - 2 * d
            t_copy(slot, t_core_sem.at[2 * d - 1], mate).wait_send()
            if d < line - 1:

                @pl.when(has_up)
                def _():
                    t_copy(slot, t_up_sem.at[d], i + 2).wait_send()

        @pl.when(p + d < line)
        def _(d=d):
            slot = i + 2 * d
            t_copy(slot, t_core_sem.at[2 * d], mate).wait_send()
            if d < line - 1:

                @pl.when(has_down)
                def _():
                    t_copy(slot, t_down_sem.at[d], i - 2).wait_send()


def local(
    ndp,
    ngroup,
    attended,
    cotangent,
    weight,
    weight_first,
    weight_second,
    bias,
    layer_scale,
    small_first,
    small_second,
    teacher_weight,
    teacher_bias,
    teacher_scale,
    teacher_attended,
    teacher_resid,
):
    total = attended.shape[0] * ndp * ngroup
    rows, width = weight.shape
    line = ndp // 2
    half = line // 2
    wide = width // PIECES
    extra = max(1, (ngroup // PIECES).bit_length() - 1)
    dma = pltpu.SemaphoreType.DMA
    hbm = pl.BlockSpec(memory_space=pltpu.HBM)
    vmem = pl.BlockSpec(memory_space=pltpu.VMEM)
    limit = 60 * 1024 * 1024

    def like(array, dtype=None):
        return jax.ShapeDtypeStruct(array.shape, dtype or array.dtype)

    summed, sums, branch = pl.pallas_call(
        functools.partial(exchange, ndp, ngroup),
        out_shape=(
            jax.ShapeDtypeStruct((rows, width), F32),
            jax.ShapeDtypeStruct((2, width), F32),
            like(teacher_resid, F32),
        ),
        in_specs=[hbm] * 5,
        out_specs=[vmem] * 3,
        scratch_shapes=[
            pltpu.VMEM((rows, width), F32),
            pltpu.VMEM((rows, width), F32),
            pltpu.VMEM(attended.shape, BF16),
            pltpu.VMEM(cotangent.shape, BF16),
            pltpu.VMEM(teacher_attended.shape, BF16),
            dma((5,)),
            pltpu.VMEM((ndp, rows, width), BF16),
            pltpu.VMEM((2, PIECES, line, rows, wide), BF16),
            pltpu.VMEM((PIECES, line, rows, wide), BF16),
            pltpu.VMEM((PIECES, line, rows, wide), F32),
            pltpu.VMEM((PIECES, line, rows, wide), BF16),
            pltpu.VMEM((2, half, rows, wide), BF16),
            pltpu.VMEM((2, half, rows, wide), BF16),
            pltpu.VMEM((half, rows, wide), BF16),
            pltpu.VMEM((half, rows, wide), BF16),
            pltpu.VMEM((half, rows, wide), BF16),
            pltpu.VMEM((half, rows, wide), BF16),
            pltpu.VMEM((extra, line, rows, wide), BF16),
            pltpu.VMEM((extra, line, rows, wide), BF16),
            pltpu.VMEM((line, rows, wide), BF16),
            pltpu.VMEM((line - 1, rows, wide), BF16),
            pltpu.VMEM((PIECES, rows, wide), BF16),
            pltpu.VMEM((ngroup, 8, width), F32),
            pltpu.VMEM((ndp, 1, width), F32),
            pltpu.VMEM((ndp, 1, wide), F32),
            pltpu.VMEM((PIECES, 1, wide), F32),
            dma((2 * line,)),
            dma((line,)),
            dma((line,)),
            dma((ndp,)),
            dma((PIECES,)),
            dma((PIECES,)),
            dma((6,)),
            dma((6,)),
            dma((extra,)),
            dma((extra,)),
            dma((line - 1,)),
            dma((line - 1,)),
            dma((PIECES - 1,)),
            dma((PIECES - 1,)),
            dma((ngroup,)),
            dma((ngroup,)),
            dma((ndp - 1,)),
            dma((ndp - 1,)),
            dma((ndp - 1,)),
            dma((ndp - 1,)),
            dma((PIECES - 1,)),
            dma((PIECES - 1,)),
        ],
        compiler_params=pltpu.CompilerParams(
            collective_id=0, has_side_effects=True, vmem_limit_bytes=limit
        ),
    )(weight, teacher_weight, attended, cotangent, teacher_attended)
    large = [like(weight)] * 5
    little = [like(small_first)] * 5
    out_shape = (*large, *little, like(teacher_resid))
    return pl.pallas_call(
        functools.partial(finish, total),
        out_shape=out_shape,
        in_specs=[vmem] * 14,
        out_specs=[hbm] * 11,
        scratch_shapes=[pltpu.VMEM(o.shape, o.dtype) for o in out_shape] + [dma((11, 3))],
        compiler_params=pltpu.CompilerParams(vmem_limit_bytes=limit),
    )(
        summed,
        sums,
        branch,
        weight,
        weight_first,
        weight_second,
        bias,
        layer_scale,
        small_first,
        small_second,
        teacher_weight,
        teacher_bias,
        teacher_scale,
        teacher_resid,
    )


def solution(mesh):
    placed = (
        P(("dp", "group"), None),
        P(("dp", "group"), None),
        P("dp", None),
        P("dp", None),
        P("dp", None),
        P(),
        P(),
        P(),
        P(),
        P("dp", None),
        P(),
        P(),
        P(("dp", "group"), None),
        P(("dp", "group"), None),
    )
    return jax.shard_map(
        functools.partial(local, mesh.shape["dp"], mesh.shape["group"]),
        mesh=mesh,
        in_specs=placed,
        out_specs=(
            P("dp", None),
            P("dp", None),
            P("dp", None),
            P("dp", None),
            P("dp", None),
            P(),
            P(),
            P(),
            P(),
            P(),
            P(("dp", "group"), None),
        ),
        check_vma=False,
    )
```

```python
import functools

import jax
import jax.numpy as jnp
from jax import lax
from jax.experimental import pallas as pl
from jax.experimental.pallas import tpu as pltpu
from jax.sharding import PartitionSpec as P

BETA_ONE = 0.9
BETA_TWO = 0.999
LEARN_RATE = 0.0004
WEIGHT_DECAY = 0.04
EPSILON = 1e-08
MOMENTUM = 0.994
CORRECT_ONE = 1.0 - 0.9**10
CORRECT_TWO = 1.0 - 0.999**10
PIECES = 4
F32 = jnp.float32
BF16 = jnp.bfloat16


def adam_update(param, first, second, grad, decay):
    first = BETA_ONE * first + (1.0 - BETA_ONE) * grad
    second = BETA_TWO * second + (1.0 - BETA_TWO) * grad * grad
    direction = first / CORRECT_ONE / (jnp.sqrt(second / CORRECT_TWO) + EPSILON) + decay * param
    return (param - LEARN_RATE * direction, first, second, direction)


def finish(
    total,
    grad_ref,
    sums_ref,
    branch_ref,
    weight_ref,
    first_ref,
    second_ref,
    bias_ref,
    scale_ref,
    small_first_ref,
    small_second_ref,
    tweight_ref,
    tbias_ref,
    tscale_ref,
    tres_ref,
    *rest,
):
    outs, held, sem = rest[:11], rest[11:22], rest[22]
    rows, width = weight_ref.shape
    chunk = rows // 3 if rows % 24 == 0 else rows
    chunks = rows // chunk
    copies = []

    def send(n, where=None, k=0):
        src, dst = held[n], outs[n]
        if where is not None:
            src, dst = src.at[where], dst.at[where]
        copy = pltpu.make_async_copy(src, dst, sem.at[n, k])
        copy.start()
        copies.append(copy)

    scale = scale_ref[...][None, :]
    for k in range(chunks):
        where = pl.ds(k * chunk, chunk)
        grad = grad_ref[where] * scale / total
        param = weight_ref[where]
        held[4][where] = MOMENTUM * tweight_ref[where] + (1.0 - MOMENTUM) * param
        results = adam_update(param, first_ref[where], second_ref[where], grad, WEIGHT_DECAY)
        for n, result in enumerate(results):
            held[n][where] = result
        for n in range(5):
            send(n, where, k)
    bias = bias_ref[...][None, :]
    small = (bias, scale)
    bias_sum = sums_ref[0:1]
    scale_sum = sums_ref[1:2] + bias * bias_sum
    small_grad = (scale * bias_sum / total, scale_sum / total)
    blended = []
    for r, old in enumerate((tbias_ref, tscale_ref)):
        row = pl.ds(r, 1)
        results = adam_update(
            small[r], small_first_ref[row], small_second_ref[row], small_grad[r], 0.0
        )
        blended.append(MOMENTUM * old[...][None, :] + (1.0 - MOMENTUM) * small[r])
        for n, result in enumerate((*results, blended[r])):
            held[5 + n][row] = result
    for n in range(5, 10):
        send(n)
    held[10][...] = (
        tres_ref[...].astype(F32) + blended[1] * (branch_ref[...] + blended[0])
    ).astype(BF16)
    send(10)
    for copy in copies:
        copy.wait()


def exchange(
    ndp,
    ngroup,
    weight_hbm,
    tweight_hbm,
    att_hbm,
    cot_hbm,
    tatt_hbm,
    grad_ref,
    sums_ref,
    branch_ref,
    weight,
    tweight,
    att,
    cot,
    tatt,
    load_sem,
    tgather,
    part,
    from_core,
    acc,
    narrow,
    got_a,
    got_b,
    send_a,
    send_b,
    last_a,
    last_b,
    extra_out,
    extra_in,
    z_out,
    z_in,
    pieces,
    bias_slots,
    bias_all,
    scale_slots,
    scale_pieces,
    t_core_sem,
    t_up_sem,
    t_down_sem,
    t_recv,
    core_send,
    core_recv,
    plane_send,
    plane_recv,
    extra_send,
    extra_recv,
    z_send,
    z_recv,
    piece_send,
    piece_recv,
    bias_send,
    bias_recv,
    bias_all_send,
    bias_all_recv,
    scale_send,
    scale_recv,
    scale_piece_send,
    scale_piece_recv,
):
    line = ndp // 2
    half = line // 2
    i = lax.axis_index("dp")
    g = lax.axis_index("group")
    p = i // 2
    c = i % 2
    own = g % PIECES
    rows, width = weight.shape
    wide = width // PIECES

    def flip(index, bits):
        out = index
        bit = 1
        while bit <= bits:
            if bits & bit:
                out = out + bit - 2 * bit * ((index // bit) % 2)
            bit *= 2
        return out

    def remote(src, dst, send_sem, recv_sem, dp, group):
        return pltpu.make_async_remote_copy(
            src_ref=src,
            dst_ref=dst,
            send_sem=send_sem,
            recv_sem=recv_sem,
            device_id=(dp, group),
            device_id_type=pl.DeviceIdType.MESH,
        )

    loads = [
        pltpu.make_async_copy(src, dst, load_sem.at[k])
        for k, (src, dst) in enumerate(
            [
                (weight_hbm, weight),
                (tweight_hbm, tweight),
                (att_hbm, att),
                (cot_hbm, cot),
                (tatt_hbm, tatt),
            ]
        )
    ]
    for load in loads:
        load.start()

    barrier = pltpu.get_barrier_semaphore()
    for k in range(1, ndp):
        pl.semaphore_signal(
            barrier, inc=1, device_id=(flip(i, k), g), device_id_type=pl.DeviceIdType.MESH
        )
    for k in range(1, ngroup):
        pl.semaphore_signal(
            barrier, inc=1, device_id=(i, flip(g, k)), device_id_type=pl.DeviceIdType.MESH
        )

    loads[0].wait()
    loads[1].wait()
    tgather[i] = (MOMENTUM * tweight[...] + (1.0 - MOMENTUM) * weight[...]).astype(BF16)
    pl.semaphore_wait(barrier, ndp - 1 + ngroup - 1)

    def t_copy(slot, send_sem, dp):
        return remote(tgather.at[slot], tgather.at[slot], send_sem, t_recv.at[slot], dp, g)

    mate = flip(i, 1)
    up = jnp.minimum(i + 2, ndp - 1)
    down = jnp.maximum(i - 2, 0)
    has_up = p < line - 1
    has_down = p > 0

    @pl.when(has_up)
    def _():
        t_copy(i, t_up_sem.at[0], i + 2).start()

    @pl.when(has_down)
    def _():
        t_copy(i, t_down_sem.at[0], i - 2).start()

    t_copy(i, t_core_sem.at[0], mate).start()

    def forward(d):
        @pl.when(p - d >= 0)
        def _():
            slot = i - 2 * d
            t_copy(slot, t_core_sem.at[2 * d - 1], mate).wait_recv()
            t_copy(slot, t_core_sem.at[2 * d - 1], mate).start()
            if d < line - 1:

                @pl.when(has_up)
                def _():
                    t_copy(slot, t_up_sem.at[d], i + 2).start()

        @pl.when(p + d < line)
        def _():
            slot = i + 2 * d
            t_copy(slot, t_core_sem.at[2 * d], mate).wait_recv()
            t_copy(slot, t_core_sem.at[2 * d], mate).start()
            if d < line - 1:

                @pl.when(has_down)
                def _():
                    t_copy(slot, t_down_sem.at[d], i - 2).start()

    loads[2].wait()
    turned = att[...].T
    loads[3].wait()

    order = [3, 1, 2, 0]
    core_copies = []
    for k in order:
        q = flip(own, k)
        columns = pl.ds(pl.multiple_of(q * wide, wide), wide)
        product = jnp.dot(turned, cot[:, columns], preferred_element_type=F32)
        product = product.reshape(line, 2, rows, wide).astype(BF16)
        part[0, q] = product[:, 0]
        part[1, q] = product[:, 1]
        copy = remote(
            part.at[1 - c, q], from_core.at[q], core_send.at[k], core_recv.at[k], mate, g
        )
        copy.start()
        core_copies.append(copy)

    ones = jnp.ones((8, cot.shape[0]), BF16)
    bias_slots[g] = jnp.dot(ones, cot[...], preferred_element_type=F32)
    bias_copies = [
        remote(
            bias_slots.at[g], bias_slots.at[g], bias_send.at[k], bias_recv.at[k], i, flip(g, k)
        )
        for k in range(1, ngroup)
    ]
    for copy in bias_copies:
        copy.start()

    x_mate = flip(g, 1)
    y_mate = flip(g, 2)
    quarter = half // 2
    low = [pl.ds(h * quarter, quarter) for h in range(2)]
    high = [pl.ds(half + h * quarter, quarter) for h in range(2)]

    def plane(n, src, dst, group):
        return remote(src, dst, plane_send.at[n], plane_recv.at[n], i, group)

    plane_copies = []
    for h in range(2):
        plane_copies += [
            plane(6 * h, narrow.at[flip(own, 3), low[h]], got_a.at[h, 0], x_mate),
            plane(6 * h + 1, narrow.at[flip(own, 3), high[h]], got_b.at[h, 0], y_mate),
            plane(6 * h + 2, narrow.at[flip(own, 1), low[h]], got_a.at[h, 1], x_mate),
            plane(6 * h + 3, narrow.at[flip(own, 2), high[h]], got_b.at[h, 1], y_mate),
            plane(6 * h + 4, send_a.at[h], last_a.at[h], y_mate),
            plane(6 * h + 5, send_b.at[h], last_b.at[h], x_mate),
        ]
    after = {3: (0, 1), 1: (2,), 2: (3,), 0: (6, 7, 8, 9)}
    for n, k in enumerate(order):
        q = flip(own, k)
        core_copies[n].wait_recv()
        total = part[c, q].astype(F32) + from_core[q].astype(F32)
        acc[q] = total
        if k != 0:
            narrow[q] = total.astype(BF16)
        for m in after[k]:
            plane_copies[m].start()

    for copy in bias_copies:
        copy.wait_recv()
    bias_total = bias_slots[0, 0:1]
    for k in range(1, ngroup):
        bias_total = bias_total + bias_slots[k, 0:1]
    bias_all[i] = bias_total
    bias_all_copies = [
        remote(
            bias_all.at[i],
            bias_all.at[i],
            bias_all_send.at[k - 1],
            bias_all_recv.at[k - 1],
            flip(i, k),
            g,
        )
        for k in range(1, ndp)
    ]
    for copy in bias_all_copies:
        copy.start()

    def second(h):
        plane_copies[6 * h].wait_recv()
        send_a[h] = (acc[flip(own, 2), low[h]] + got_a[h, 0].astype(F32)).astype(BF16)
        plane_copies[6 * h + 4].start()
        plane_copies[6 * h + 1].wait_recv()
        send_b[h] = (acc[flip(own, 1), high[h]] + got_b[h, 0].astype(F32)).astype(BF16)
        plane_copies[6 * h + 5].start()

    def third(h):
        plane_copies[6 * h + 2].wait_recv()
        plane_copies[6 * h + 4].wait_recv()
        acc[own, low[h]] = acc[own, low[h]] + (got_a[h, 1].astype(F32) + last_a[h].astype(F32))
        plane_copies[6 * h + 3].wait_recv()
        plane_copies[6 * h + 5].wait_recv()
        acc[own, high[h]] = acc[own, high[h]] + (got_b[h, 1].astype(F32) + last_b[h].astype(F32))

    def z_copy(place, k):
        return remote(
            z_out.at[place], z_in.at[k - 1], z_send.at[k - 1], z_recv.at[k - 1], 2 * place + c, g
        )

    def to_line(h):
        for first in (h * quarter, half + h * quarter):
            where = pl.ds(first, quarter)
            z_out[where] = acc[own, where].astype(BF16)
            for place in range(first, first + quarter):

                @pl.when(p != place)
                def _(place=place):
                    z_copy(place, flip(p, place)).start()

    second(0)
    forward(1)
    second(1)
    third(0)
    if ngroup == PIECES:
        to_line(0)
    third(1)

    extra_copies = []
    step = 0
    while PIECES << step < ngroup:
        extra_out[step] = acc[own].astype(BF16)
        copy = remote(
            extra_out.at[step],
            extra_in.at[step],
            extra_send.at[step],
            extra_recv.at[step],
            i,
            flip(g, PIECES << step),
        )
        copy.start()
        copy.wait_recv()
        acc[own] = extra_out[step].astype(F32) + extra_in[step].astype(F32)
        extra_copies.append(copy)
        step += 1

    if ngroup != PIECES:
        to_line(0)
    to_line(1)
    for d in range(2, line - 1):
        forward(d)
    z_copies = [z_copy(flip(p, k), k) for k in range(1, line)]

    total = acc[own, p]
    for copy in z_copies:
        copy.wait_recv()
    for k in range(line - 1):
        total = total + z_in[k].astype(F32)
    pieces[own] = total.astype(BF16)
    piece_copies = [
        remote(
            pieces.at[own],
            pieces.at[own],
            piece_send.at[k - 1],
            piece_recv.at[k - 1],
            i,
            flip(g, k),
        )
        for k in (3, 1, 2)
    ]
    for copy in piece_copies:
        copy.start()
    columns = pl.ds(pl.multiple_of(own * wide, wide), wide)
    rounded = weight[:, columns].astype(BF16).astype(F32)
    scale_slots[i] = jnp.sum(rounded * pieces[own].astype(F32), 0, keepdims=True)
    scale_copies = [
        remote(
            scale_slots.at[i],
            scale_slots.at[i],
            scale_send.at[k - 1],
            scale_recv.at[k - 1],
            flip(i, k),
            g,
        )
        for k in range(ndp - 1, 0, -1)
    ]
    for copy in scale_copies:
        copy.start()
    if line > 2:
        forward(line - 1)
    for k in range(line):
        slot = 2 * k + 1 - c
        t_copy(slot, t_core_sem.at[0], mate).wait_recv()
    if rows % 16 == 0:
        blended_all = tgather[...].reshape(ndp * rows, width)
    else:
        blended_all = tgather[...].astype(F32).reshape(ndp * rows, width).astype(BF16)
    loads[4].wait()
    branch_ref[...] = jnp.dot(tatt[...], blended_all, preferred_element_type=F32)

    for copy in bias_all_copies:
        copy.wait_recv()
    bias_sum = bias_all[0]
    for k in range(1, ndp):
        bias_sum = bias_sum + bias_all[k]
    sums_ref[0:1] = bias_sum
    for copy in scale_copies:
        copy.wait_recv()
    scale_sum = scale_slots[0]
    for k in range(1, ndp):
        scale_sum = scale_sum + scale_slots[k]
    scale_pieces[own] = scale_sum
    scale_piece_copies = [
        remote(
            scale_pieces.at[own],
            scale_pieces.at[own],
            scale_piece_send.at[k - 1],
            scale_piece_recv.at[k - 1],
            i,
            flip(g, k),
        )
        for k in (3, 1, 2)
    ]
    for copy in scale_piece_copies:
        copy.start()
    for copy in piece_copies:
        copy.wait_recv()
    for q in range(PIECES):
        grad_ref[:, pl.ds(q * wide, wide)] = pieces[q].astype(F32)
    for copy in scale_piece_copies:
        copy.wait_recv()
    for q in range(PIECES):
        sums_ref[1:2, pl.ds(q * wide, wide)] = scale_pieces[q]

    for copy in (
        core_copies + bias_copies + plane_copies + extra_copies + z_copies + piece_copies
    ):
        copy.wait_send()
    for copy in bias_all_copies + scale_copies + scale_piece_copies:
        copy.wait_send()
    t_copy(i, t_core_sem.at[0], mate).wait_send()

    @pl.when(has_up)
    def _():
        t_copy(i, t_up_sem.at[0], i + 2).wait_send()

    @pl.when(has_down)
    def _():
        t_copy(i, t_down_sem.at[0], i - 2).wait_send()

    for d in range(1, line):

        @pl.when(p - d >= 0)
        def _(d=d):
            slot = i - 2 * d
            t_copy(slot, t_core_sem.at[2 * d - 1], mate).wait_send()
            if d < line - 1:

                @pl.when(has_up)
                def _():
                    t_copy(slot, t_up_sem.at[d], i + 2).wait_send()

        @pl.when(p + d < line)
        def _(d=d):
            slot = i + 2 * d
            t_copy(slot, t_core_sem.at[2 * d], mate).wait_send()
            if d < line - 1:

                @pl.when(has_down)
                def _():
                    t_copy(slot, t_down_sem.at[d], i - 2).wait_send()


def local(
    ndp,
    ngroup,
    attended,
    cotangent,
    weight,
    weight_first,
    weight_second,
    bias,
    layer_scale,
    small_first,
    small_second,
    teacher_weight,
    teacher_bias,
    teacher_scale,
    teacher_attended,
    teacher_resid,
):
    total = attended.shape[0] * ndp * ngroup
    rows, width = weight.shape
    line = ndp // 2
    half = line // 2
    wide = width // PIECES
    extra = max(1, (ngroup // PIECES).bit_length() - 1)
    dma = pltpu.SemaphoreType.DMA
    hbm = pl.BlockSpec(memory_space=pltpu.HBM)
    vmem = pl.BlockSpec(memory_space=pltpu.VMEM)
    limit = 60 * 1024 * 1024

    def like(array, dtype=None):
        return jax.ShapeDtypeStruct(array.shape, dtype or array.dtype)

    summed, sums, branch = pl.pallas_call(
        functools.partial(exchange, ndp, ngroup),
        out_shape=(
            jax.ShapeDtypeStruct((rows, width), F32),
            jax.ShapeDtypeStruct((2, width), F32),
            like(teacher_resid, F32),
        ),
        in_specs=[hbm] * 5,
        out_specs=[vmem] * 3,
        scratch_shapes=[
            pltpu.VMEM((rows, width), F32),
            pltpu.VMEM((rows, width), F32),
            pltpu.VMEM(attended.shape, BF16),
            pltpu.VMEM(cotangent.shape, BF16),
            pltpu.VMEM(teacher_attended.shape, BF16),
            dma((5,)),
            pltpu.VMEM((ndp, rows, width), BF16),
            pltpu.VMEM((2, PIECES, line, rows, wide), BF16),
            pltpu.VMEM((PIECES, line, rows, wide), BF16),
            pltpu.VMEM((PIECES, line, rows, wide), F32),
            pltpu.VMEM((PIECES, line, rows, wide), BF16),
            pltpu.VMEM((2, 2, half // 2, rows, wide), BF16),
            pltpu.VMEM((2, 2, half // 2, rows, wide), BF16),
            pltpu.VMEM((2, half // 2, rows, wide), BF16),
            pltpu.VMEM((2, half // 2, rows, wide), BF16),
            pltpu.VMEM((2, half // 2, rows, wide), BF16),
            pltpu.VMEM((2, half // 2, rows, wide), BF16),
            pltpu.VMEM((extra, line, rows, wide), BF16),
            pltpu.VMEM((extra, line, rows, wide), BF16),
            pltpu.VMEM((line, rows, wide), BF16),
            pltpu.VMEM((line - 1, rows, wide), BF16),
            pltpu.VMEM((PIECES, rows, wide), BF16),
            pltpu.VMEM((ngroup, 8, width), F32),
            pltpu.VMEM((ndp, 1, width), F32),
            pltpu.VMEM((ndp, 1, wide), F32),
            pltpu.VMEM((PIECES, 1, wide), F32),
            dma((2 * line,)),
            dma((line,)),
            dma((line,)),
            dma((ndp,)),
            dma((PIECES,)),
            dma((PIECES,)),
            dma((12,)),
            dma((12,)),
            dma((extra,)),
            dma((extra,)),
            dma((line - 1,)),
            dma((line - 1,)),
            dma((PIECES - 1,)),
            dma((PIECES - 1,)),
            dma((ngroup,)),
            dma((ngroup,)),
            dma((ndp - 1,)),
            dma((ndp - 1,)),
            dma((ndp - 1,)),
            dma((ndp - 1,)),
            dma((PIECES - 1,)),
            dma((PIECES - 1,)),
        ],
        compiler_params=pltpu.CompilerParams(
            collective_id=0, has_side_effects=True, vmem_limit_bytes=limit
        ),
    )(weight, teacher_weight, attended, cotangent, teacher_attended)
    large = [like(weight)] * 5
    little = [like(small_first)] * 5
    out_shape = (*large, *little, like(teacher_resid))
    return pl.pallas_call(
        functools.partial(finish, total),
        out_shape=out_shape,
        in_specs=[vmem] * 14,
        out_specs=[hbm] * 11,
        scratch_shapes=[pltpu.VMEM(o.shape, o.dtype) for o in out_shape] + [dma((11, 3))],
        compiler_params=pltpu.CompilerParams(vmem_limit_bytes=limit),
    )(
        summed,
        sums,
        branch,
        weight,
        weight_first,
        weight_second,
        bias,
        layer_scale,
        small_first,
        small_second,
        teacher_weight,
        teacher_bias,
        teacher_scale,
        teacher_resid,
    )


def solution(mesh):
    placed = (
        P(("dp", "group"), None),
        P(("dp", "group"), None),
        P("dp", None),
        P("dp", None),
        P("dp", None),
        P(),
        P(),
        P(),
        P(),
        P("dp", None),
        P(),
        P(),
        P(("dp", "group"), None),
        P(("dp", "group"), None),
    )
    return jax.shard_map(
        functools.partial(local, mesh.shape["dp"], mesh.shape["group"]),
        mesh=mesh,
        in_specs=placed,
        out_specs=(
            P("dp", None),
            P("dp", None),
            P("dp", None),
            P("dp", None),
            P("dp", None),
            P(),
            P(),
            P(),
            P(),
            P(),
            P(("dp", "group"), None),
        ),
        check_vma=False,
    )
```
